128 devices in a mesh: grp: 16 (over x_lo, y, core), freq: 8 (over x_hi, z).
Axes of the slice: x: 4 (x_hi: 2, x_lo: 2; x = x_hi * 2 + x_lo), y: 4, z: 4, core: 2. Of those that a mesh axis runs over, the one named last changes fastest.
Arguments:
- records: bfloat16 [64, 8192, 512], P(None, ('grp', 'freq')), may hold values from -60000 to 60000
- plan: int32 [2], replicated, may hold values from 1 to 15, as said below
Outputs:
- within_spectra: bfloat16 [16, 64, 10, 128, 256], P('grp', 'freq')
- round_spectra: bfloat16 [16, 2, 64, 8, 128, 256], P('grp', None, 'freq')
The draws below stay inside these ranges and needn't reach their ends.
Inputs may be any that keep to these rules, and one draw needn't show every extreme that they name: `plan`: the masks of different rounds differ.
All inputs are finite; a program needn't handle non-finite values.
Results may differ from the reference program's by a relative error of at most 0.0058.
Values may be sent and summed in bfloat16 or wider, within the bound.
A program may use at most 128 MiB of HBM per device.

```python
import jax
import jax.numpy as jnp
from jax import lax

F = 64
GSTA = 128
W = 256
GPD = 4
ROUNDS = 2
GROUPS = 64
STATIONS = 8192
N_GRP = 16


def draw_records(key, part):
    key = jax.random.fold_in(key, 11)
    key_base, key_station, key_freq, key_window = jax.random.split(key, 4)
    shape = (F, STATIONS, 2 * W)
    base = jnp.clip(jax.random.normal(key_base, shape, jnp.float32), -6.0, 6.0)
    top = 10.0
    spread = jnp.log(top)
    station_scale = jnp.exp(jax.random.uniform(key_station, (1, STATIONS, 1), jnp.float32) * spread)
    freq_scale = jnp.exp(jax.random.uniform(key_freq, (F, 1, 1), jnp.float32) * spread)
    window_scale = jnp.exp(jax.random.uniform(key_window, (1, 1, W), jnp.float32) * spread)
    window_both = jnp.concatenate([window_scale, window_scale], -1)
    return (base * station_scale * freq_scale * window_both).astype(jnp.bfloat16)


def draw_plan(key, part):
    key = jax.random.fold_in(key, 23)
    key_masks, key_order = jax.random.split(key, 2)
    others = jax.random.permutation(key_masks, N_GRP - 2)[:ROUNDS - 1] + 1
    masks = jnp.concatenate([others.astype(jnp.int32), jnp.full((1,), N_GRP - 1, jnp.int32)])
    order = jax.random.permutation(key_order, ROUNDS)
    return masks[order].astype(jnp.int32)


def setup_inputs(seed: int = 0) -> dict:
    splits = jax.random.split(jax.random.key(seed), 3)
    return {
        "records": draw_records(jax.random.fold_in(splits[2], 71), 0),
        "plan": draw_plan(jax.random.fold_in(splits[2], 71), 0),
    }


EPS = 1e-06

def pack_right(block):
    half = block.shape[-1] // 2
    turned = jnp.concatenate([-block[..., half:], block[..., :half]], -1)
    return jnp.concatenate([block, turned], -2)

def cross_spectra(left, right):
    product = jnp.einsum('flsw,frtw->flrst', left.astype(jnp.float32), pack_right(right).astype(jnp.float32), precision=lax.Precision.HIGHEST)
    scaled = product * W ** (-0.5)
    shape = scaled.shape
    return scaled.reshape(shape[0], shape[1] * shape[2], shape[3], shape[4]).astype(jnp.bfloat16)

def reference(records, plan):
    values = records.astype(jnp.float32)
    power_sum = lax.optimization_barrier(jnp.sum(values * values, -1, keepdims=True)) / W
    white = (values * lax.rsqrt(power_sum + EPS)).astype(jnp.bfloat16)
    groups = white.reshape(F, GROUPS, GSTA, 2 * W)

    def per_device(device):
        own_groups = lax.dynamic_slice_in_dim(groups, (device * GPD).astype(jnp.int32), GPD, 1)
        within = jnp.concatenate([cross_spectra(own_groups[:, first:first + 1], own_groups[:, first:]) for first in range(GPD)], 1)
        rounds_out = []
        for round_step in range(ROUNDS):
            partner_index = jnp.bitwise_xor(device, plan[round_step]).astype(jnp.int32)
            partner = lax.dynamic_slice_in_dim(groups, partner_index * GPD, GPD, 1)
            lower_part = cross_spectra(own_groups[:, :GPD // 2], partner)
            upper_part = cross_spectra(own_groups, partner[:, GPD // 2:])
            rounds_out.append(jnp.where(device < partner_index, lower_part, upper_part))
        return (within, jnp.stack(rounds_out))
    within_spectra, round_spectra = lax.map(per_device, jnp.arange(N_GRP, dtype=jnp.int32))
    return (within_spectra, round_spectra)
```

```python
import functools

import jax
import jax.numpy as jnp
from jax import lax
from jax.experimental import pallas as pl
from jax.experimental.pallas import tpu as pltpu
from jax.sharding import PartitionSpec as P

GSTA = 128
W = 256
GPD = 4
ROUNDS = 2
N_GRP = 16
EPS = 1e-06


def turned(block):
    return jnp.concatenate([-block[:, W:], block[:, :W]], -1)


def times(left, right):
    return lax.dot_general(left, right, (((1,), (1,)), ((), ())), preferred_element_type=jnp.float32)


def spectra_kernel(lower_ref, own_ref, partner_ref, within_ref, round_ref):
    own = own_ref.at[0]

    def cross(rows, right_ref, start):
        right = right_ref[pl.ds(start, GSTA), :]
        packed = jnp.concatenate([right, turned(right)], 0)
        return (times(own[pl.ds(0, rows), :], packed) * W ** (-0.5)).astype(jnp.bfloat16)

    pairs = [(i, j) for i in range(GPD) for j in range(i, GPD)]
    for j in range(GPD):
        product = cross((j + 1) * GSTA, own, j * GSTA)
        for i in range(j + 1):
            within_ref[0, 0, pairs.index((i, j))] = product[i * GSTA : (i + 1) * GSTA]
    for r in range(ROUNDS):
        partner = partner_ref.at[r, 0]

        @pl.when(lower_ref[r] == 1)
        def _():
            for j in range(GPD):
                product = cross(2 * GSTA, partner, j * GSTA)
                for i in range(2):
                    round_ref[0, r, 0, i * GPD + j] = product[i * GSTA : (i + 1) * GSTA]

        @pl.when(lower_ref[r] == 0)
        def _():
            for j in range(2):
                product = cross(GPD * GSTA, partner, (2 + j) * GSTA)
                for i in range(GPD):
                    round_ref[0, r, 0, i * 2 + j] = product[i * GSTA : (i + 1) * GSTA]


def spectra(lower, own, partner):
    freqs, stations, width = own.shape
    return pl.pallas_call(
        spectra_kernel,
        grid_spec=pltpu.PrefetchScalarGridSpec(
            num_scalar_prefetch=1,
            grid=(freqs,),
            in_specs=[
                pl.BlockSpec((1, stations, width), lambda f, _: (f, 0, 0)),
                pl.BlockSpec((ROUNDS, 1, stations, width), lambda f, _: (0, f, 0, 0)),
            ],
            out_specs=[
                pl.BlockSpec((1, 1, 10, GSTA, 2 * GSTA), lambda f, _: (0, f, 0, 0, 0)),
                pl.BlockSpec((1, ROUNDS, 1, 8, GSTA, 2 * GSTA), lambda f, _: (0, 0, f, 0, 0, 0)),
            ],
        ),
        out_shape=[
            jax.ShapeDtypeStruct((1, freqs, 10, GSTA, 2 * GSTA), jnp.bfloat16),
            jax.ShapeDtypeStruct((1, ROUNDS, freqs, 8, GSTA, 2 * GSTA), jnp.bfloat16),
        ],
        compiler_params=pltpu.CompilerParams(vmem_limit_bytes=48 * 1024 * 1024),
        cost_estimate=pl.CostEstimate(flops=7 * 10**9, bytes_accessed=27 * 10**6, transcendentals=0),
        name="spectra",
    )(lower, own, partner)


def fetch(own, mask):
    def by(m):
        return lambda: lax.ppermute(own, "grp", [(i, i ^ m) for i in range(N_GRP)])

    return lax.switch(mask - 1, [by(m) for m in range(1, N_GRP)])


def body(records, plan):
    regrouped = lax.all_to_all(records, "freq", split_axis=0, concat_axis=1, tiled=True)
    values = regrouped.astype(jnp.float32)
    power_sum = jnp.sum(values * values, -1, keepdims=True) / W
    white = (values * lax.rsqrt(power_sum + EPS)).astype(jnp.bfloat16)
    me = lax.axis_index("grp")
    partner = jnp.stack([fetch(white, plan[r]) for r in range(ROUNDS)])
    lower = (me < jnp.bitwise_xor(me, plan)).astype(jnp.int32)
    within, rounds = spectra(lower, white, partner)
    return within, rounds


def solution(mesh):
    placed = (P(None, ("grp", "freq"), None), P())
    return jax.shard_map(
        body,
        mesh=mesh,
        in_specs=placed,
        out_specs=(P("grp", "freq", None, None, None), P("grp", None, "freq", None, None, None)),
        check_vma=False,
    )
```

```python
import functools

import jax
import jax.numpy as jnp
from jax import lax
from jax.experimental import pallas as pl
from jax.experimental.pallas import tpu as pltpu
from jax.sharding import PartitionSpec as P

GSTA = 128
W = 256
GPD = 4
ROUNDS = 2
N_GRP = 16
EPS = 1e-06


def turned(block):
    return jnp.concatenate([-block[:, W:], block[:, :W]], -1)


def times(left, right):
    return lax.dot_general(left, right, (((1,), (1,)), ((), ())), preferred_element_type=jnp.float32)


def spectra_kernel(lower_ref, own_ref, partner_ref, within_ref, round_ref):
    own = own_ref.at[0]

    def cross(rows, right_ref, start):
        right = right_ref[pl.ds(start, GSTA), :]
        packed = jnp.concatenate([right, turned(right)], 0)
        return (times(own[pl.ds(0, rows), :], packed) * W ** (-0.5)).astype(jnp.bfloat16)

    pairs = [(i, j) for i in range(GPD) for j in range(i, GPD)]
    for j in range(GPD):
        product = cross((j + 1) * GSTA, own, j * GSTA)
        for i in range(j + 1):
            within_ref[0, 0, pairs.index((i, j))] = product[i * GSTA : (i + 1) * GSTA]
    for r in range(ROUNDS):
        partner = partner_ref.at[r, 0]

        @pl.when(lower_ref[r] == 1)
        def _():
            for j in range(GPD):
                product = cross(2 * GSTA, partner, j * GSTA)
                for i in range(2):
                    round_ref[0, r, 0, i * GPD + j] = product[i * GSTA : (i + 1) * GSTA]

        @pl.when(lower_ref[r] == 0)
        def _():
            for j in range(2):
                product = cross(GPD * GSTA, partner, (2 + j) * GSTA)
                for i in range(GPD):
                    round_ref[0, r, 0, i * 2 + j] = product[i * GSTA : (i + 1) * GSTA]


def spectra(lower, own, partner):
    freqs, stations, width = own.shape
    return pl.pallas_call(
        spectra_kernel,
        grid_spec=pltpu.PrefetchScalarGridSpec(
            num_scalar_prefetch=1,
            grid=(freqs,),
            in_specs=[
                pl.BlockSpec((1, stations, width), lambda f, _: (f, 0, 0)),
                pl.BlockSpec((ROUNDS, 1, stations, width), lambda f, _: (0, f, 0, 0)),
            ],
            out_specs=[
                pl.BlockSpec((1, 1, 10, GSTA, 2 * GSTA), lambda f, _: (0, f, 0, 0, 0)),
                pl.BlockSpec((1, ROUNDS, 1, 8, GSTA, 2 * GSTA), lambda f, _: (0, 0, f, 0, 0, 0)),
            ],
        ),
        out_shape=[
            jax.ShapeDtypeStruct((1, freqs, 10, GSTA, 2 * GSTA), jnp.bfloat16),
            jax.ShapeDtypeStruct((1, ROUNDS, freqs, 8, GSTA, 2 * GSTA), jnp.bfloat16),
        ],
        compiler_params=pltpu.CompilerParams(vmem_limit_bytes=48 * 1024 * 1024),
        cost_estimate=pl.CostEstimate(flops=7 * 10**9, bytes_accessed=27 * 10**6, transcendentals=0),
        name="spectra",
    )(lower, own, partner)

X_LO = 8
X_HI = 4


def flip(index, size):
    return index + size - 2 * size * (index // size % 2)


def meet(index, bits, size):
    for bit in (1, 2):
        if bits & bit:
            index = flip(index, size * bit)
    return index


def exchange_kernel(
    hops, plan_ref, rec_ref, own_ref, got_ref, ready, across, blocks, picked,
    z_out, z_in, x_out, x_in, core_out, core_in, y_out, y_in, own_sem,
):
    chunks, _, _, stations, _ = blocks.shape
    part = rec_ref.shape[1]
    half = stations // 2
    g = lax.axis_index("grp")
    q = lax.axis_index("freq")
    z = q % 4
    hi = q // X_HI
    inner = (flip(g, X_LO), q)
    outer = (flip(g, X_LO), flip(q, X_HI))
    mate = (flip(g, 1), q)
    aside = [(g, meet(q, j, 1)) for j in range(1, 4)]
    along = [(meet(g, hop, 2), q) for hop in hops]
    friends = [inner, outer, mate] + aside
    friends += [along[r] for r in range(ROUNDS) if hops[r] and hops[r] not in hops[:r]]

    barrier = pltpu.get_barrier_semaphore()
    for friend in friends:
        pl.semaphore_signal(barrier, inc=1, device_id=friend, device_id_type=pl.DeviceIdType.MESH)
    pl.semaphore_wait(barrier, len(friends))

    near = pl.ds(pl.multiple_of(hi * half, half), half)
    far = pl.ds(pl.multiple_of((1 - hi) * half, half), half)
    near_part = pl.ds(pl.multiple_of(hi * half + z * part, part), part)
    far_part = pl.ds(pl.multiple_of(z * part, part), part)

    def remote(source, target, sent, landed, device):
        return pltpu.make_async_remote_copy(
            src_ref=source, dst_ref=target, send_sem=sent, recv_sem=landed,
            device_id=device, device_id_type=pl.DeviceIdType.MESH,
        )

    def z_copies(c):
        copies = []
        for j in range(3):
            copies.append(remote(
                ready.at[c, j, 0], blocks.at[c, 0, 0, near_part],
                z_out.at[c, j, 0], z_in.at[c, j, 0], aside[j],
            ))
            copies.append(remote(
                ready.at[c, j, 1], across.at[c, far_part],
                z_out.at[c, j, 1], z_in.at[c, j, 1], aside[j],
            ))
        return copies

    def x_inner(c):
        return remote(
            blocks.at[c, 0, 0, near], blocks.at[c, 0, 1, near], x_out.at[c, 0], x_in.at[c, 0], inner
        )

    def x_outer(c):
        return remote(across.at[c], blocks.at[c, 0, 1, near], x_out.at[c, 1], x_in.at[c, 1], outer)

    def x_relay(c):
        return remote(
            blocks.at[c, 0, 1, far], blocks.at[c, 0, 0, far], x_out.at[c, 2], x_in.at[c, 2], inner
        )

    def core_copy(c):
        return remote(blocks.at[c, 0], blocks.at[c, 1], core_out.at[c], core_in.at[c], mate)

    def own_copy(c):
        return pltpu.make_async_copy(blocks.at[c, 0, 0], own_ref.at[c], own_sem.at[c])

    def y_copy(c, r):
        if hops[r]:
            return remote(
                picked.at[r, c], got_ref.at[r, c], y_out.at[r, c], y_in.at[r, c], along[r]
            )
        return pltpu.make_async_copy(picked.at[r, c], got_ref.at[r, c], y_out.at[r, c])

    def whiten(c):
        for j in range(4):
            for k in range(2):
                band = (hi if k == 0 else 1 - hi) * X_HI + meet(z, j, 1)
                values = rec_ref[band * chunks + c].astype(jnp.float32)
                power = jnp.sum(values * values, -1, keepdims=True) / W
                white = (values * lax.rsqrt(power + EPS)).astype(jnp.bfloat16)
                if j:
                    ready[c, j - 1, k] = white
                elif k:
                    across[c, far_part] = white
                else:
                    blocks[c, 0, 0, near_part] = white
        for copy in z_copies(c):
            copy.start()

    def spread(c):
        for copy in z_copies(c):
            copy.wait_recv()
        x_inner(c).start()
        x_outer(c).start()

    def relay(c):
        x_outer_landed(c).wait_recv()
        x_relay(c).start()

    def x_outer_landed(c):
        return remote(across.at[c], blocks.at[c, 0, 1, far], x_out.at[c, 1], x_in.at[c, 1], outer)

    def share(c):
        x_inner_landed = remote(
            blocks.at[c, 0, 0, near], blocks.at[c, 0, 1, near], x_out.at[c, 0], x_in.at[c, 0], inner
        )
        x_inner_landed.wait_recv()
        x_relay(c).wait_recv()
        core_copy(c).start()
        own_copy(c).start()

    def send(c):
        core_copy(c).wait_recv()
        for r in range(ROUNDS):
            other_lo = plan_ref[r] >= X_LO
            other_core = plan_ref[r] % 2 == 1
            here = jnp.where(other_lo, blocks[c, 0, 1], blocks[c, 0, 0])
            there = jnp.where(other_lo, blocks[c, 1, 1], blocks[c, 1, 0])
            picked[r, c] = jnp.where(other_core, there, here)
        for r in range(ROUNDS):
            y_copy(c, r).start()

    def step(t, carry):
        for stage, late in ((spread, 1), (whiten, 0), (relay, 2), (send, 4), (share, 3)):
            pl.when((t >= late) & (t < chunks + late))(functools.partial(stage, t - late))
        return carry

    lax.fori_loop(0, chunks + 4, step, 0)

    def finish(c, carry):
        for copy in z_copies(c) + [x_inner(c), x_outer(c), x_relay(c), core_copy(c)]:
            copy.wait_send()
        own_copy(c).wait()
        for r in range(ROUNDS):
            y_copy(c, r).wait()
        return carry

    lax.fori_loop(0, chunks, finish, 0)


def exchange(records, plan, hops):
    freqs, part, width = records.shape
    bands = 8
    chunks = freqs // bands
    stations = part * bands
    block = (stations, width)
    dma = pltpu.SemaphoreType.DMA
    return pl.pallas_call(
        functools.partial(exchange_kernel, hops),
        out_shape=[
            jax.ShapeDtypeStruct((chunks,) + block, jnp.bfloat16),
            jax.ShapeDtypeStruct((ROUNDS, chunks) + block, jnp.bfloat16),
        ],
        in_specs=[pl.BlockSpec(memory_space=pltpu.SMEM), pl.BlockSpec(memory_space=pltpu.VMEM)],
        out_specs=[pl.BlockSpec(memory_space=pl.ANY)] * 2,
        scratch_shapes=[
            pltpu.VMEM((chunks, 3, 2, part, width), jnp.bfloat16),
            pltpu.VMEM((chunks, stations // 2, width), jnp.bfloat16),
            pltpu.VMEM((chunks, 2, 2) + block, jnp.bfloat16),
            pltpu.VMEM((ROUNDS, chunks) + block, jnp.bfloat16),
            dma((chunks, 3, 2)), dma((chunks, 3, 2)), dma((chunks, 3)), dma((chunks, 3)),
            dma((chunks,)), dma((chunks,)), dma((ROUNDS, chunks)), dma((ROUNDS, chunks)),
            dma((chunks,)),
        ],
        compiler_params=pltpu.CompilerParams(
            collective_id=1 + hops[0] * 4 + hops[1], has_side_effects=True,
            vmem_limit_bytes=52 * 1024 * 1024,
        ),
        name="exchange_%d%d" % hops,
    )(plan, records)


def body(records, plan):
    branches = [
        functools.partial(exchange, hops=(first, second)) for first in range(4) for second in range(4)
    ]
    hop = plan // 2 % 4
    own, got = lax.switch(hop[0] * 4 + hop[1], branches, records, plan)
    me = lax.axis_index("grp")
    lower = (me < jnp.bitwise_xor(me, plan)).astype(jnp.int32)
    within, rounds = spectra(lower, own, got)
    return within, rounds


def solution(mesh):
    placed = (P(None, ("grp", "freq"), None), P())
    return jax.shard_map(
        body,
        mesh=mesh,
        in_specs=placed,
        out_specs=(P("grp", "freq", None, None, None), P("grp", None, "freq", None, None, None)),
        check_vma=False,
    )
```

```python
import functools

import jax
import jax.numpy as jnp
from jax import lax
from jax.experimental import pallas as pl
from jax.experimental.pallas import tpu as pltpu
from jax.sharding import PartitionSpec as P

GSTA = 128
W = 256
GPD = 4
ROUNDS = 2
N_GRP = 16
EPS = 1e-06


def turned(block):
    return jnp.concatenate([-block[:, W:], block[:, :W]], -1)


def times(left, right):
    return lax.dot_general(left, right, (((1,), (1,)), ((), ())), preferred_element_type=jnp.float32)


def spectra_kernel(plan_ref, own_ref, partner_ref, within_ref, round_ref):
    own = own_ref.at[0]
    me = lax.axis_index("grp")

    def cross(rows, right_ref, start):
        right = right_ref[pl.ds(start, GSTA), :]
        packed = jnp.concatenate([right, turned(right)], 0)
        return (times(own[pl.ds(0, rows), :], packed) * W ** (-0.5)).astype(jnp.bfloat16)

    pairs = [(i, j) for i in range(GPD) for j in range(i, GPD)]
    for j in range(GPD):
        product = cross((j + 1) * GSTA, own, j * GSTA)
        for i in range(j + 1):
            within_ref[0, 0, pairs.index((i, j))] = product[i * GSTA : (i + 1) * GSTA]
    for r in range(ROUNDS):
        partner = partner_ref.at[r, 0]
        lower = me < jnp.bitwise_xor(me, plan_ref[r])

        @pl.when(lower)
        def _():
            for j in range(GPD):
                product = cross(2 * GSTA, partner, j * GSTA)
                for i in range(2):
                    round_ref[0, r, 0, i * GPD + j] = product[i * GSTA : (i + 1) * GSTA]

        @pl.when(jnp.logical_not(lower))
        def _():
            for j in range(2):
                product = cross(GPD * GSTA, partner, (2 + j) * GSTA)
                for i in range(GPD):
                    round_ref[0, r, 0, i * 2 + j] = product[i * GSTA : (i + 1) * GSTA]


def spectra(plan, own, partner):
    freqs, stations, width = own.shape
    return pl.pallas_call(
        spectra_kernel,
        grid_spec=pltpu.PrefetchScalarGridSpec(
            num_scalar_prefetch=1,
            grid=(freqs,),
            in_specs=[
                pl.BlockSpec((1, stations, width), lambda f, _: (f, 0, 0)),
                pl.BlockSpec((ROUNDS, 1, stations, width), lambda f, _: (0, f, 0, 0)),
            ],
            out_specs=[
                pl.BlockSpec((1, 1, 10, GSTA, 2 * GSTA), lambda f, _: (0, f, 0, 0, 0)),
                pl.BlockSpec((1, ROUNDS, 1, 8, GSTA, 2 * GSTA), lambda f, _: (0, 0, f, 0, 0, 0)),
            ],
        ),
        out_shape=[
            jax.ShapeDtypeStruct((1, freqs, 10, GSTA, 2 * GSTA), jnp.bfloat16),
            jax.ShapeDtypeStruct((1, ROUNDS, freqs, 8, GSTA, 2 * GSTA), jnp.bfloat16),
        ],
        compiler_params=pltpu.CompilerParams(vmem_limit_bytes=48 * 1024 * 1024),
        cost_estimate=pl.CostEstimate(flops=7 * 10**9, bytes_accessed=27 * 10**6, transcendentals=0),
        name="spectra",
    )(plan, own, partner)

X_LO = 8
X_HI = 4
BANDS = 8
SLICES = 2


def flip(index, size):
    return index + size - 2 * size * (index // size % 2)


def meet(index, bits, size):
    for bit in (1, 2):
        if bits & bit:
            index = flip(index, size * bit)
    return index


def exchange_kernel(
    hops, pass_on, plan_ref, rec_ref, own_ref, got_ref, raw, ready, across, blocks, picked,
    raw_sem, z_out, z_in, x_out, x_in, core_out, core_in, y_out, y_in, own_sem,
):
    chunks = blocks.shape[0]
    half = BANDS // 2
    g = lax.axis_index("grp")
    q = lax.axis_index("freq")
    z = q % 4
    hi = q // X_HI
    inner = (flip(g, X_LO), q)
    outer = (flip(g, X_LO), flip(q, X_HI))
    mate = (flip(g, 1), q)
    aside = [(g, meet(q, j, 1)) for j in range(1, 4)]
    along = [(meet(g, hop, 2), q) for hop in hops]
    sends = [r for r in range(ROUNDS) if not (pass_on and pass_on[1] == r)]
    friends = [inner, outer, mate] + aside + [along[r] for r in sends if hops[r]]
    if pass_on:
        first, second, turn, swap = pass_on
        onward = (meet(flip(g, 1) if swap else g, turn, 2), q)
        friends.append(onward)

    def raw_copy(c):
        return pltpu.make_async_copy(rec_ref.at[:, c], raw.at[c], raw_sem.at[c])

    def load(c, carry):
        raw_copy(c).start()
        return carry

    lax.fori_loop(0, chunks, load, 0)

    barrier = pltpu.get_barrier_semaphore()
    for friend in friends:
        pl.semaphore_signal(barrier, inc=1, device_id=friend, device_id_type=pl.DeviceIdType.MESH)
    pl.semaphore_wait(barrier, len(friends))

    near = pl.ds(hi * half, half)
    far = pl.ds((1 - hi) * half, half)

    def remote(source, target, sent, landed, device):
        return pltpu.make_async_remote_copy(
            src_ref=source, dst_ref=target, send_sem=sent, recv_sem=landed,
            device_id=device, device_id_type=pl.DeviceIdType.MESH,
        )

    def z_copies(c):
        copies = []
        for j in range(3):
            copies.append(remote(
                ready.at[c, j, 0], blocks.at[c, 0, 0, hi * half + z],
                z_out.at[c, j, 0], z_in.at[c, j, 0], aside[j],
            ))
            copies.append(remote(
                ready.at[c, j, 1], across.at[c, z],
                z_out.at[c, j, 1], z_in.at[c, j, 1], aside[j],
            ))
        return copies

    def x_inner(c):
        return remote(
            blocks.at[c, 0, 0, near], blocks.at[c, 0, 1, near], x_out.at[c, 0], x_in.at[c, 0], inner
        )

    def x_outer(c, rows):
        return remote(across.at[c], blocks.at[c, 0, 1, rows], x_out.at[c, 1], x_in.at[c, 1], outer)

    def x_relay(c):
        return remote(
            blocks.at[c, 0, 1, far], blocks.at[c, 0, 0, far], x_out.at[c, 2], x_in.at[c, 2], inner
        )

    def core_copy(c):
        return remote(blocks.at[c, 0], blocks.at[c, 1], core_out.at[c], core_in.at[c], mate)

    def own_copy(c):
        return pltpu.make_async_copy(
            blocks.at[c, 0, 0], own_ref.at[c // SLICES, :, c % SLICES], own_sem.at[c]
        )

    def landing(c, r):
        return got_ref.at[r, c // SLICES, :, c % SLICES]

    def y_copy(c, r):
        if hops[r]:
            return remote(
                picked.at[r, c], landing(c, r), y_out.at[r, c], y_in.at[r, c], along[r]
            )
        return pltpu.make_async_copy(picked.at[r, c], landing(c, r), y_out.at[r, c])

    def onward_copy(c):
        return remote(
            landing(c, first), landing(c, second), y_out.at[second, c], y_in.at[second, c], onward
        )

    def whiten(c):
        raw_copy(c).wait()
        for j in range(4):
            for k in range(2):
                band = (hi if k == 0 else 1 - hi) * half + meet(z, j, 1)
                values = raw[c, band].astype(jnp.float32)
                power = jnp.sum(values * values, -1, keepdims=True) / W
                white = (values * lax.rsqrt(power + EPS)).astype(jnp.bfloat16)
                if j:
                    ready[c, j - 1, k] = white
                elif k:
                    across[c, z] = white
                else:
                    blocks[c, 0, 0, hi * half + z] = white
        for copy in z_copies(c):
            copy.start()

    def spread(c):
        for copy in z_copies(c):
            copy.wait_recv()
        x_inner(c).start()
        x_outer(c, near).start()

    def relay(c):
        x_outer(c, far).wait_recv()
        x_relay(c).start()

    def share(c):
        x_inner(c).wait_recv()
        x_relay(c).wait_recv()
        core_copy(c).start()
        own_copy(c).start()

    def send(c):
        core_copy(c).wait_recv()
        for r in sends:
            other_lo = plan_ref[r] >= X_LO
            other_core = plan_ref[r] % 2 == 1
            here = jnp.where(other_lo, blocks[c, 0, 1], blocks[c, 0, 0])
            there = jnp.where(other_lo, blocks[c, 1, 1], blocks[c, 1, 0])
            picked[r, c] = jnp.where(other_core, there, here)
            y_copy(c, r).start()

    def hand_on(c):
        y_copy(c, first).wait_recv()
        onward_copy(c).start()

    stages = [(spread, 1), (whiten, 0), (relay, 2), (send, 4), (share, 3)]
    if pass_on:
        stages.append((hand_on, 6))

    def step(t, carry):
        for stage, late in stages:
            pl.when((t >= late) & (t < chunks + late))(functools.partial(stage, t - late))
        return carry

    lax.fori_loop(0, chunks + max(late for _, late in stages), step, 0)

    def finish(c, carry):
        for copy in z_copies(c) + [x_inner(c), x_outer(c, near), x_relay(c), core_copy(c)]:
            copy.wait_send()
        own_copy(c).wait()
        for r in sends:
            if pass_on and r == first:
                y_copy(c, r).wait_send()
            else:
                y_copy(c, r).wait()
        if pass_on:
            onward_copy(c).wait()
        return carry

    lax.fori_loop(0, chunks, finish, 0)


def exchange(records, plan, variant, number):
    freqs, stations, width = records.shape
    chunks = freqs // BANDS * SLICES
    part = (stations // SLICES, width)
    block = (BANDS,) + part
    dma = pltpu.SemaphoreType.DMA
    own, got = pl.pallas_call(
        functools.partial(exchange_kernel, *variant),
        out_shape=[
            jax.ShapeDtypeStruct((freqs // BANDS, BANDS, SLICES) + part, jnp.bfloat16),
            jax.ShapeDtypeStruct((ROUNDS, freqs // BANDS, BANDS, SLICES) + part, jnp.bfloat16),
        ],
        in_specs=[pl.BlockSpec(memory_space=pltpu.SMEM), pl.BlockSpec(memory_space=pl.ANY)],
        out_specs=[pl.BlockSpec(memory_space=pl.ANY)] * 2,
        scratch_shapes=[
            pltpu.VMEM((chunks,) + block, jnp.bfloat16),
            pltpu.VMEM((chunks, 3, 2) + part, jnp.bfloat16),
            pltpu.VMEM((chunks, BANDS // 2) + part, jnp.bfloat16),
            pltpu.VMEM((chunks, 2, 2) + block, jnp.bfloat16),
            pltpu.VMEM((ROUNDS, chunks) + block, jnp.bfloat16),
            dma((chunks,)),
            dma((chunks, 3, 2)), dma((chunks, 3, 2)), dma((chunks, 3)), dma((chunks, 3)),
            dma((chunks,)), dma((chunks,)), dma((ROUNDS, chunks)), dma((ROUNDS, chunks)),
            dma((chunks,)),
        ],
        compiler_params=pltpu.CompilerParams(
            collective_id=1 + number, has_side_effects=True, vmem_limit_bytes=52 * 1024 * 1024
        ),
        name="exchange_%d" % number,
    )(plan, records.reshape((BANDS, chunks) + part))
    shape = (freqs // BANDS, stations * BANDS, width)
    return own.reshape(shape), got.reshape((ROUNDS,) + shape)


def variants():
    found = [((first, second), None) for first in range(4) for second in range(4)]
    found += [((hop, hop), (0, 1, 0, 1)) for hop in (1, 2, 3)]
    for swap in range(2):
        for first, second in ((1, 2), (2, 1), (2, 3), (3, 2)):
            order = (1, 0) if first == 2 else (0, 1)
            odd = second if first == 2 else first
            found.append(((first, second), order + (2 ^ odd, swap)))
    return found


def variant_number(plan):
    first, second = plan[0] >> 1 & 3, plan[1] >> 1 & 3
    change = plan[0] ^ plan[1]
    both = first * second
    direct = (first << 2) + second
    turned_off = 19 + ((change & 1) << 2) + jnp.minimum((direct >> 1) - 3, 3)
    relayed = jnp.where(first == second, 15 + first, turned_off)
    return jnp.where((change < X_LO) & (both != 0) & (both != 3), relayed, direct)


def body(records, plan):
    branches = [
        functools.partial(exchange, variant=variant, number=number)
        for number, variant in enumerate(variants())
    ]
    own, got = lax.switch(variant_number(plan), branches, records, plan)
    return spectra(plan, own, got)


def solution(mesh):
    placed = (P(None, ("grp", "freq"), None), P())
    return jax.shard_map(
        body,
        mesh=mesh,
        in_specs=placed,
        out_specs=(P("grp", "freq", None, None, None), P("grp", None, "freq", None, None, None)),
        check_vma=False,
    )
```

```python
import functools

import jax
import jax.numpy as jnp
from jax import lax
from jax.experimental import pallas as pl
from jax.experimental.pallas import tpu as pltpu
from jax.sharding import PartitionSpec as P

GSTA = 128
W = 256
GPD = 4
ROUNDS = 2
N_GRP = 16
EPS = 1e-06


def turned(block):
    return jnp.concatenate([-block[:, W:], block[:, :W]], -1)


def times(left, right):
    return lax.dot_general(left, right, (((1,), (1,)), ((), ())), preferred_element_type=jnp.float32)


def group_pairs():
    return [(i, j) for i in range(GPD) for j in range(i, GPD)]


def cross(left, right):
    packed = jnp.concatenate([right, turned(right)], 0)
    return (times(left, packed) * W ** (-0.5)).astype(jnp.bfloat16)


def hop_of(mask):
    return mask >> 1 & 3


def swapped_slots(plan):
    return (hop_of(plan[0]) > hop_of(plan[1])).astype(jnp.int32)


def spectra_kernel(plan_ref, own_ref, partner_ref, inside_ref, within_ref, round_ref):
    own = own_ref.at[0]
    me = lax.axis_index("grp")
    swapped = swapped_slots(plan_ref)
    within_ref[0] = inside_ref[...]
    for r in range(ROUNDS):
        partner = partner_ref.at[swapped if r == 0 else 1 - swapped, 0]
        lower = me < jnp.bitwise_xor(me, plan_ref[r])

        @pl.when(lower)
        def _():
            for j in range(GPD):
                product = cross(own[pl.ds(0, 2 * GSTA), :], partner[pl.ds(j * GSTA, GSTA), :])
                for i in range(2):
                    round_ref[0, r, 0, i * GPD + j] = product[i * GSTA : (i + 1) * GSTA]

        @pl.when(jnp.logical_not(lower))
        def _():
            for j in range(2):
                product = cross(own[...], partner[pl.ds((2 + j) * GSTA, GSTA), :])
                for i in range(GPD):
                    round_ref[0, r, 0, i * 2 + j] = product[i * GSTA : (i + 1) * GSTA]


def spectra(plan, own, partner, inside):
    freqs, stations, width = own.shape
    pairs = inside.shape[1:]
    return pl.pallas_call(
        spectra_kernel,
        grid_spec=pltpu.PrefetchScalarGridSpec(
            num_scalar_prefetch=1,
            grid=(freqs,),
            in_specs=[
                pl.BlockSpec((1, stations, width), lambda f, _: (f, 0, 0)),
                pl.BlockSpec((ROUNDS, 1, stations, width), lambda f, _: (0, f, 0, 0)),
                pl.BlockSpec((1,) + pairs, lambda f, _: (f, 0, 0, 0)),
            ],
            out_specs=[
                pl.BlockSpec((1, 1) + pairs, lambda f, _: (0, f, 0, 0, 0)),
                pl.BlockSpec((1, ROUNDS, 1, 8, GSTA, 2 * GSTA), lambda f, _: (0, 0, f, 0, 0, 0)),
            ],
        ),
        out_shape=[
            jax.ShapeDtypeStruct((1, freqs) + pairs, jnp.bfloat16),
            jax.ShapeDtypeStruct((1, ROUNDS, freqs, 8, GSTA, 2 * GSTA), jnp.bfloat16),
        ],
        compiler_params=pltpu.CompilerParams(vmem_limit_bytes=32 * 1024 * 1024),
        cost_estimate=pl.CostEstimate(flops=5 * 10**9, bytes_accessed=32 * 10**6, transcendentals=0),
        name="spectra",
    )(plan, own, partner, inside)


X_LO = 8
X_HI = 4
BANDS = 8
SLICES = 2


def flip(index, size):
    return index + size - 2 * size * (index // size % 2)


def meet(index, bits, size):
    for bit in (1, 2):
        if bits & bit:
            index = flip(index, size * bit)
    return index


def exchange_kernel(
    hops, pass_on, plan_ref, rec_ref, own_ref, got_ref, inside_ref,
    raw, ready, across, blocks, picked, mine, inside,
    raw_sem, z_out, z_in, x_out, x_in, core_out, core_in, y_out, y_in, own_sem, inside_sem,
):
    chunks = blocks.shape[0]
    swapped = swapped_slots(plan_ref)
    masks = [plan_ref[swapped], plan_ref[1 - swapped]]
    half = BANDS // 2
    g = lax.axis_index("grp")
    q = lax.axis_index("freq")
    z = q % 4
    hi = q // X_HI
    inner = (flip(g, X_LO), q)
    outer = (flip(g, X_LO), flip(q, X_HI))
    mate = (flip(g, 1), q)
    aside = [(g, meet(q, j, 1)) for j in range(1, 4)]
    along = [(meet(g, hop, 2), q) for hop in hops]
    sends = [r for r in range(ROUNDS) if not (pass_on and pass_on[1] == r)]
    friends = [inner, outer, mate] + aside + [along[r] for r in sends if hops[r]]
    if pass_on:
        first, second, turn, swap = pass_on
        onward = (meet(flip(g, 1) if swap else g, turn, 2), q)
        friends.append(onward)

    def raw_copy(c):
        return pltpu.make_async_copy(rec_ref.at[:, c], raw.at[c], raw_sem.at[c])

    def load(c, carry):
        raw_copy(c).start()
        return carry

    lax.fori_loop(0, chunks, load, 0)

    barrier = pltpu.get_barrier_semaphore()
    for friend in friends:
        pl.semaphore_signal(barrier, inc=1, device_id=friend, device_id_type=pl.DeviceIdType.MESH)
    pl.semaphore_wait(barrier, len(friends))

    near = pl.ds(hi * half, half)
    far = pl.ds((1 - hi) * half, half)

    def remote(source, target, sent, landed, device):
        return pltpu.make_async_remote_copy(
            src_ref=source, dst_ref=target, send_sem=sent, recv_sem=landed,
            device_id=device, device_id_type=pl.DeviceIdType.MESH,
        )

    def z_copies(c):
        copies = []
        for j in range(3):
            copies.append(remote(
                ready.at[c, j, 0], blocks.at[c, 0, 0, hi * half + z],
                z_out.at[c, j, 0], z_in.at[c, j, 0], aside[j],
            ))
            copies.append(remote(
                ready.at[c, j, 1], across.at[c, z],
                z_out.at[c, j, 1], z_in.at[c, j, 1], aside[j],
            ))
        return copies

    def x_inner(c):
        return remote(
            blocks.at[c, 0, 0, near], blocks.at[c, 0, 1, near], x_out.at[c, 0], x_in.at[c, 0], inner
        )

    def x_outer(c, rows):
        return remote(across.at[c], blocks.at[c, 0, 1, rows], x_out.at[c, 1], x_in.at[c, 1], outer)

    def x_relay(c):
        return remote(
            blocks.at[c, 0, 1, far], blocks.at[c, 0, 0, far], x_out.at[c, 2], x_in.at[c, 2], inner
        )

    def core_copy(c):
        return remote(blocks.at[c, 0], blocks.at[c, 1], core_out.at[c], core_in.at[c], mate)

    def own_copy(c):
        return pltpu.make_async_copy(
            blocks.at[c, 0, 0], own_ref.at[c // SLICES, :, c % SLICES], own_sem.at[c]
        )

    def landing(c, r):
        return got_ref.at[r, c // SLICES, :, c % SLICES]

    def y_copy(c, r):
        if hops[r]:
            return remote(
                picked.at[r, c], landing(c, r), y_out.at[r, c], y_in.at[r, c], along[r]
            )
        return pltpu.make_async_copy(picked.at[r, c], landing(c, r), y_out.at[r, c])

    def onward_copy(c):
        return remote(
            landing(c, first), landing(c, second), y_out.at[second, c], y_in.at[second, c], onward
        )

    def whiten(c):
        raw_copy(c).wait()
        for j in range(4):
            for k in range(2):
                band = (hi if k == 0 else 1 - hi) * half + meet(z, j, 1)
                values = raw[c, band].astype(jnp.float32)
                power = jnp.sum(values * values, -1, keepdims=True) / W
                white = (values * lax.rsqrt(power + EPS)).astype(jnp.bfloat16)
                if j:
                    ready[c, j - 1, k] = white
                elif k:
                    across[c, z] = white
                else:
                    blocks[c, 0, 0, hi * half + z] = white
        for copy in z_copies(c):
            copy.start()

    def spread(c):
        for copy in z_copies(c):
            copy.wait_recv()
        x_inner(c).start()
        x_outer(c, near).start()

    def relay(c):
        x_outer(c, far).wait_recv()
        x_relay(c).start()

    def share(c):
        x_inner(c).wait_recv()
        x_relay(c).wait_recv()
        core_copy(c).start()
        own_copy(c).start()

    def send(c):
        core_copy(c).wait_recv()
        for r in sends:
            other_lo = masks[r] >= X_LO
            other_core = masks[r] % 2 == 1
            here = jnp.where(other_lo, blocks[c, 0, 1], blocks[c, 0, 0])
            there = jnp.where(other_lo, blocks[c, 1, 1], blocks[c, 1, 0])
            picked[r, c] = jnp.where(other_core, there, here)
            y_copy(c, r).start()

    def hand_on(c):
        y_copy(c, first).wait_recv()
        onward_copy(c).start()

    def inside_copy(f):
        return pltpu.make_async_copy(inside.at[f], inside_ref.at[f], inside_sem.at[f])

    def pair_up(c):
        f = c // SLICES
        part = blocks.shape[-2]
        for p in range(BANDS):
            for piece in range(SLICES):
                start = (p * SLICES + piece) * part
                mine[start : start + part] = blocks[f * SLICES + piece, 0, 0, p]
        pairs = group_pairs()
        for j in range(GPD):
            product = cross(mine[: (j + 1) * GSTA], mine[j * GSTA : (j + 1) * GSTA])
            for i in range(j + 1):
                inside[f, pairs.index((i, j))] = product[i * GSTA : (i + 1) * GSTA]
        inside_copy(f).start()

    stages = [(whiten, 0), (spread, 1), (relay, 2), (share, 3), (send, 3)]
    if pass_on:
        stages.append((hand_on, 5))

    def step(t, carry):
        for stage, late in stages:
            pl.when((t >= late) & (t < chunks + late))(functools.partial(stage, t - late))
        done = t - 3
        pl.when((done >= 0) & (done < chunks) & (done % SLICES == SLICES - 1))(
            functools.partial(pair_up, done)
        )
        return carry

    lax.fori_loop(0, chunks + max(late for _, late in stages), step, 0)

    def finish(c, carry):
        for copy in z_copies(c) + [x_inner(c), x_outer(c, near), x_relay(c), core_copy(c)]:
            copy.wait_send()
        own_copy(c).wait()
        pl.when(c % SLICES == 0)(lambda: inside_copy(c // SLICES).wait())
        for r in sends:
            if pass_on and r == first:
                y_copy(c, r).wait_send()
            else:
                y_copy(c, r).wait()
        if pass_on:
            onward_copy(c).wait()
        return carry

    lax.fori_loop(0, chunks, finish, 0)


def exchange(records, plan, variant, number):
    freqs, stations, width = records.shape
    chunks = freqs // BANDS * SLICES
    part = (stations // SLICES, width)
    block = (BANDS,) + part
    dma = pltpu.SemaphoreType.DMA
    pairs = (len(group_pairs()), GSTA, 2 * GSTA)
    own, got, inside = pl.pallas_call(
        functools.partial(exchange_kernel, *variant),
        out_shape=[
            jax.ShapeDtypeStruct((freqs // BANDS, BANDS, SLICES) + part, jnp.bfloat16),
            jax.ShapeDtypeStruct((ROUNDS, freqs // BANDS, BANDS, SLICES) + part, jnp.bfloat16),
            jax.ShapeDtypeStruct((freqs // BANDS,) + pairs, jnp.bfloat16),
        ],
        in_specs=[pl.BlockSpec(memory_space=pltpu.SMEM), pl.BlockSpec(memory_space=pl.ANY)],
        out_specs=[pl.BlockSpec(memory_space=pl.ANY)] * 3,
        scratch_shapes=[
            pltpu.VMEM((chunks,) + block, jnp.bfloat16),
            pltpu.VMEM((chunks, 3, 2) + part, jnp.bfloat16),
            pltpu.VMEM((chunks, BANDS // 2) + part, jnp.bfloat16),
            pltpu.VMEM((chunks, 2, 2) + block, jnp.bfloat16),
            pltpu.VMEM((ROUNDS, chunks) + block, jnp.bfloat16),
            pltpu.VMEM((stations * BANDS, width), jnp.bfloat16),
            pltpu.VMEM((freqs // BANDS,) + pairs, jnp.bfloat16),
            dma((chunks,)),
            dma((chunks, 3, 2)), dma((chunks, 3, 2)), dma((chunks, 3)), dma((chunks, 3)),
            dma((chunks,)), dma((chunks,)), dma((ROUNDS, chunks)), dma((ROUNDS, chunks)),
            dma((chunks,)), dma((freqs // BANDS,)),
        ],
        compiler_params=pltpu.CompilerParams(
            collective_id=1 + number, has_side_effects=True, vmem_limit_bytes=46 * 1024 * 1024
        ),
        name="exchange_%d" % number,
    )(plan, records.reshape((BANDS, chunks) + part))
    shape = (freqs // BANDS, stations * BANDS, width)
    return own.reshape(shape), got.reshape((ROUNDS,) + shape), inside


def variants():
    found = [((low, high), None) for high in range(4) for low in range(high + 1)]
    found += [((hop, hop), (0, 1, 0, 1)) for hop in (1, 2, 3)]
    found += [((1, 2), (0, 1, 3, swap)) for swap in range(2)]
    found += [((2, 3), (1, 0, 1, swap)) for swap in range(2)]
    return found


def variant_number(plan):
    first, second = hop_of(plan[0]), hop_of(plan[1])
    low, high = jnp.minimum(first, second), jnp.maximum(first, second)
    change = plan[0] ^ plan[1]
    direct = (high * (high + 1) >> 1) + low
    turned_off = 13 + ((high & 1) << 1) + (change & 1)
    relayed = jnp.where(low == high, 9 + high, turned_off)
    return jnp.where((change < X_LO) & (low != 0) & (low * high != 3), relayed, direct)


def body(records, plan):
    branches = [
        functools.partial(exchange, variant=variant, number=number)
        for number, variant in enumerate(variants())
    ]
    return spectra(plan, *lax.switch(variant_number(plan), branches, records, plan))


def solution(mesh):
    placed = (P(None, ("grp", "freq"), None), P())
    return jax.shard_map(
        body,
        mesh=mesh,
        in_specs=placed,
        out_specs=(P("grp", "freq", None, None, None), P("grp", None, "freq", None, None, None)),
        check_vma=False,
    )
```

```python
import functools

import jax
import jax.numpy as jnp
from jax import lax
from jax.experimental import pallas as pl
from jax.experimental.pallas import tpu as pltpu
from jax.sharding import PartitionSpec as P

GSTA = 128
W = 256
GPD = 4
ROUNDS = 2
N_GRP = 16
EPS = 1e-06


def turned(block):
    return jnp.concatenate([-block[:, W:], block[:, :W]], -1)


def times(left, right):
    return lax.dot_general(left, right, (((1,), (1,)), ((), ())), preferred_element_type=jnp.float32)


def group_pairs():
    return [(i, j) for i in range(GPD) for j in range(i, GPD)]


def cross(left, right):
    packed = jnp.concatenate([right, turned(right)], 0)
    return (times(left, packed) * W ** (-0.5)).astype(jnp.bfloat16)


def hop_of(mask):
    return mask >> 1 & 3


def swapped_slots(plan):
    return (hop_of(plan[0]) > hop_of(plan[1])).astype(jnp.int32)


def spectra_kernel(
    plan_ref, own_ref, got_ref, inside_ref, within_ref, round_ref, staged, within_sem, round_sem
):
    freqs = own_ref.shape[0]
    me = lax.axis_index("grp")
    swapped = swapped_slots(plan_ref)
    within_copy = pltpu.make_async_copy(inside_ref, within_ref.at[0], within_sem)
    within_copy.start()

    def round_copy(f, r):
        return pltpu.make_async_copy(staged.at[r, f], round_ref.at[0, r, f], round_sem.at[r, f])

    def make(f, carry):
        own = own_ref.at[f]
        for r in range(ROUNDS):
            partner = got_ref.at[swapped if r == 0 else 1 - swapped, f]
            lower = me < jnp.bitwise_xor(me, plan_ref[r])

            @pl.when(lower)
            def _():
                for j in range(GPD):
                    product = cross(own[pl.ds(0, 2 * GSTA), :], partner[pl.ds(j * GSTA, GSTA), :])
                    for i in range(2):
                        staged[r, f, i * GPD + j] = product[i * GSTA : (i + 1) * GSTA]

            @pl.when(jnp.logical_not(lower))
            def _():
                for j in range(2):
                    product = cross(own[...], partner[pl.ds((2 + j) * GSTA, GSTA), :])
                    for i in range(GPD):
                        staged[r, f, i * 2 + j] = product[i * GSTA : (i + 1) * GSTA]

            round_copy(f, r).start()
        return carry

    def finish(f, carry):
        for r in range(ROUNDS):
            round_copy(f, r).wait()
        return carry

    lax.fori_loop(0, freqs, make, 0)
    lax.fori_loop(0, freqs, finish, 0)
    within_copy.wait()


def spectra(plan, own, got, inside):
    freqs = own.shape[0]
    rounds = (ROUNDS, freqs, 8, GSTA, 2 * GSTA)
    dma = pltpu.SemaphoreType.DMA
    return pl.pallas_call(
        spectra_kernel,
        in_specs=[pl.BlockSpec(memory_space=pltpu.SMEM)] + [pl.BlockSpec(memory_space=pltpu.VMEM)] * 3,
        out_specs=[pl.BlockSpec(memory_space=pl.ANY)] * 2,
        out_shape=[
            jax.ShapeDtypeStruct((1,) + inside.shape, jnp.bfloat16),
            jax.ShapeDtypeStruct((1,) + rounds, jnp.bfloat16),
        ],
        scratch_shapes=[pltpu.VMEM(rounds, jnp.bfloat16), dma, dma((ROUNDS, freqs))],
        compiler_params=pltpu.CompilerParams(vmem_limit_bytes=36 * 1024 * 1024),
        cost_estimate=pl.CostEstimate(flops=5 * 10**9, bytes_accessed=14 * 10**6, transcendentals=0),
        name="spectra",
    )(plan, own, got, inside)


X_LO = 8
X_HI = 4
BANDS = 8
SLICES = 2


def flip(index, size):
    return index + size - 2 * size * (index // size % 2)


def meet(index, bits, size):
    for bit in (1, 2):
        if bits & bit:
            index = flip(index, size * bit)
    return index


def exchange_kernel(
    hops, pass_on, plan_ref, rec_ref, own_ref, got_ref, inside_ref,
    raw, ready, across, blocks, picked, mine, inside,
    raw_sem, z_out, z_in, x_out, x_in, core_out, core_in, y_out, y_in, own_sem, inside_sem,
):
    chunks = blocks.shape[0]
    swapped = swapped_slots(plan_ref)
    masks = [plan_ref[swapped], plan_ref[1 - swapped]]
    half = BANDS // 2
    g = lax.axis_index("grp")
    q = lax.axis_index("freq")
    z = q % 4
    hi = q // X_HI
    inner = (flip(g, X_LO), q)
    outer = (flip(g, X_LO), flip(q, X_HI))
    mate = (flip(g, 1), q)
    aside = [(g, meet(q, j, 1)) for j in range(1, 4)]
    along = [(meet(g, hop, 2), q) for hop in hops]
    sends = [r for r in range(ROUNDS) if not (pass_on and pass_on[1] == r)]
    friends = [inner, outer, mate] + aside + [along[r] for r in sends if hops[r]]
    if pass_on:
        first, second, turn, swap = pass_on
        onward = (meet(flip(g, 1) if swap else g, turn, 2), q)
        friends.append(onward)

    def raw_copy(c):
        return pltpu.make_async_copy(rec_ref.at[:, c], raw.at[c], raw_sem.at[c])

    def load(c, carry):
        raw_copy(c).start()
        return carry

    lax.fori_loop(0, chunks, load, 0)

    barrier = pltpu.get_barrier_semaphore()
    for friend in friends:
        pl.semaphore_signal(barrier, inc=1, device_id=friend, device_id_type=pl.DeviceIdType.MESH)
    pl.semaphore_wait(barrier, len(friends))

    near = pl.ds(hi * half, half)
    far = pl.ds((1 - hi) * half, half)

    def remote(source, target, sent, landed, device):
        return pltpu.make_async_remote_copy(
            src_ref=source, dst_ref=target, send_sem=sent, recv_sem=landed,
            device_id=device, device_id_type=pl.DeviceIdType.MESH,
        )

    def z_copies(c):
        copies = []
        for j in range(3):
            copies.append(remote(
                ready.at[c, j, 0], blocks.at[c, 0, 0, hi * half + z],
                z_out.at[c, j, 0], z_in.at[c, j, 0], aside[j],
            ))
            copies.append(remote(
                ready.at[c, j, 1], across.at[c, z],
                z_out.at[c, j, 1], z_in.at[c, j, 1], aside[j],
            ))
        return copies

    def x_inner(c):
        return remote(
            blocks.at[c, 0, 0, near], blocks.at[c, 0, 1, near], x_out.at[c, 0], x_in.at[c, 0], inner
        )

    def x_outer(c, rows):
        return remote(across.at[c], blocks.at[c, 0, 1, rows], x_out.at[c, 1], x_in.at[c, 1], outer)

    def x_relay(c):
        return remote(
            blocks.at[c, 0, 1, far], blocks.at[c, 0, 0, far], x_out.at[c, 2], x_in.at[c, 2], inner
        )

    def core_copy(c):
        return remote(blocks.at[c, 0], blocks.at[c, 1], core_out.at[c], core_in.at[c], mate)

    def own_copy(c):
        return pltpu.make_async_copy(
            blocks.at[c, 0, 0], own_ref.at[c // SLICES, :, c % SLICES], own_sem.at[c]
        )

    def landing(c, r):
        return got_ref.at[r, c // SLICES, :, c % SLICES]

    def y_copy(c, r):
        if hops[r]:
            return remote(
                picked.at[r, c], landing(c, r), y_out.at[r, c], y_in.at[r, c], along[r]
            )
        return pltpu.make_async_copy(picked.at[r, c], landing(c, r), y_out.at[r, c])

    def onward_copy(c):
        return remote(
            landing(c, first), landing(c, second), y_out.at[second, c], y_in.at[second, c], onward
        )

    def whiten(c):
        raw_copy(c).wait()
        for j in range(4):
            for k in range(2):
                band = (hi if k == 0 else 1 - hi) * half + meet(z, j, 1)
                values = raw[c, band].astype(jnp.float32)
                power = jnp.sum(values * values, -1, keepdims=True) / W
                white = (values * lax.rsqrt(power + EPS)).astype(jnp.bfloat16)
                if j:
                    ready[c, j - 1, k] = white
                elif k:
                    across[c, z] = white
                else:
                    blocks[c, 0, 0, hi * half + z] = white
        for copy in z_copies(c):
            copy.start()

    def spread(c):
        for copy in z_copies(c):
            copy.wait_recv()
        x_inner(c).start()
        x_outer(c, near).start()

    def relay(c):
        x_outer(c, far).wait_recv()
        x_relay(c).start()

    def share(c):
        x_inner(c).wait_recv()
        x_relay(c).wait_recv()
        core_copy(c).start()
        own_copy(c).start()

    def send(c):
        core_copy(c).wait_recv()
        for r in sends:
            other_lo = masks[r] >= X_LO
            other_core = masks[r] % 2 == 1
            here = jnp.where(other_lo, blocks[c, 0, 1], blocks[c, 0, 0])
            there = jnp.where(other_lo, blocks[c, 1, 1], blocks[c, 1, 0])
            picked[r, c] = jnp.where(other_core, there, here)
            y_copy(c, r).start()

    def hand_on(c):
        y_copy(c, first).wait_recv()
        onward_copy(c).start()

    def inside_copy(f):
        return pltpu.make_async_copy(inside.at[f], inside_ref.at[f], inside_sem.at[f])

    def pair_up(c):
        f = c // SLICES
        part = blocks.shape[-2]
        for p in range(BANDS):
            for piece in range(SLICES):
                start = (p * SLICES + piece) * part
                mine[start : start + part] = blocks[f * SLICES + piece, 0, 0, p]
        pairs = group_pairs()
        for j in range(GPD):
            product = cross(mine[: (j + 1) * GSTA], mine[j * GSTA : (j + 1) * GSTA])
            for i in range(j + 1):
                inside[f, pairs.index((i, j))] = product[i * GSTA : (i + 1) * GSTA]
        inside_copy(f).start()

    stages = [(whiten, 0), (relay, 2), (spread, 1), (share, 3), (send, 3)]
    if pass_on:
        stages.append((hand_on, 5))

    def step(t, carry):
        for stage, late in stages:
            pl.when((t >= late) & (t < chunks + late))(functools.partial(stage, t - late))
        done = t - 3
        pl.when((done >= 0) & (done < chunks) & (done % SLICES == SLICES - 1))(
            functools.partial(pair_up, done)
        )
        return carry

    lax.fori_loop(0, chunks + max(late for _, late in stages), step, 0)

    def finish(c, carry):
        for copy in z_copies(c) + [x_inner(c), x_outer(c, near), x_relay(c), core_copy(c)]:
            copy.wait_send()
        own_copy(c).wait()
        pl.when(c % SLICES == 0)(lambda: inside_copy(c // SLICES).wait())
        for r in sends:
            if pass_on and r == first:
                y_copy(c, r).wait_send()
            else:
                y_copy(c, r).wait()
        if pass_on:
            onward_copy(c).wait()
        return carry

    lax.fori_loop(0, chunks, finish, 0)


def exchange(records, plan, variant, number):
    freqs, stations, width = records.shape
    chunks = freqs // BANDS * SLICES
    part = (stations // SLICES, width)
    block = (BANDS,) + part
    dma = pltpu.SemaphoreType.DMA
    pairs = (len(group_pairs()), GSTA, 2 * GSTA)
    own, got, inside = pl.pallas_call(
        functools.partial(exchange_kernel, *variant),
        out_shape=[
            jax.ShapeDtypeStruct((freqs // BANDS, BANDS, SLICES) + part, jnp.bfloat16),
            jax.ShapeDtypeStruct((ROUNDS, freqs // BANDS, BANDS, SLICES) + part, jnp.bfloat16),
            jax.ShapeDtypeStruct((freqs // BANDS,) + pairs, jnp.bfloat16),
        ],
        in_specs=[pl.BlockSpec(memory_space=pltpu.SMEM), pl.BlockSpec(memory_space=pl.ANY)],
        out_specs=[pl.BlockSpec(memory_space=pl.ANY)] * 3,
        scratch_shapes=[
            pltpu.VMEM((chunks,) + block, jnp.bfloat16),
            pltpu.VMEM((chunks, 3, 2) + part, jnp.bfloat16),
            pltpu.VMEM((chunks, BANDS // 2) + part, jnp.bfloat16),
            pltpu.VMEM((chunks, 2, 2) + block, jnp.bfloat16),
            pltpu.VMEM((ROUNDS, chunks) + block, jnp.bfloat16),
            pltpu.VMEM((stations * BANDS, width), jnp.bfloat16),
            pltpu.VMEM((freqs // BANDS,) + pairs, jnp.bfloat16),
            dma((chunks,)),
            dma((chunks, 3, 2)), dma((chunks, 3, 2)), dma((chunks, 3)), dma((chunks, 3)),
            dma((chunks,)), dma((chunks,)), dma((ROUNDS, chunks)), dma((ROUNDS, chunks)),
            dma((chunks,)), dma((freqs // BANDS,)),
        ],
        compiler_params=pltpu.CompilerParams(
            collective_id=1 + number, has_side_effects=True, vmem_limit_bytes=46 * 1024 * 1024
        ),
        name="exchange_%d" % number,
    )(plan, records.reshape((BANDS, chunks) + part))
    shape = (freqs // BANDS, stations * BANDS, width)
    return own.reshape(shape), got.reshape((ROUNDS,) + shape), inside


def variants():
    found = [((low, high), None) for high in range(4) for low in range(high + 1)]
    found += [((hop, hop), (0, 1, 0, 1)) for hop in (1, 2, 3)]
    found += [((1, 2), (0, 1, 3, swap)) for swap in range(2)]
    found += [((2, 3), (1, 0, 1, swap)) for swap in range(2)]
    return found


def variant_number(plan):
    other = jnp.flip(plan)
    first, second = hop_of(plan), hop_of(other)
    low, high = jnp.minimum(first, second), jnp.maximum(first, second)
    change = plan ^ other
    direct = (high * (high + 1) >> 1) + low
    turned_off = 13 + ((high & 1) << 1) + (change & 1)
    relayed = jnp.where(low == high, 9 + high, turned_off)
    return jnp.where((change < X_LO) & (low != 0) & (low * high != 3), relayed, direct)[0]


def body(records, plan):
    branches = [
        functools.partial(exchange, variant=variant, number=number)
        for number, variant in enumerate(variants())
    ]
    return spectra(plan, *lax.switch(variant_number(plan), branches, records, plan))


def solution(mesh):
    placed = (P(None, ("grp", "freq"), None), P())
    return jax.shard_map(
        body,
        mesh=mesh,
        in_specs=placed,
        out_specs=(P("grp", "freq", None, None, None), P("grp", None, "freq", None, None, None)),
        check_vma=False,
    )
```

```python
import functools

import jax
import jax.numpy as jnp
from jax import lax
from jax.experimental import pallas as pl
from jax.experimental.pallas import tpu as pltpu
from jax.sharding import PartitionSpec as P

GSTA = 128
W = 256
GPD = 4
ROUNDS = 2
N_GRP = 16
EPS = 1e-06


def turned(block):
    return jnp.concatenate([-block[:, W:], block[:, :W]], -1)


def times(left, right):
    return lax.dot_general(left, right, (((1,), (1,)), ((), ())), preferred_element_type=jnp.float32)


def group_pairs():
    return [(i, j) for i in range(GPD) for j in range(i, GPD)]


def cross(left, right):
    packed = jnp.concatenate([right, turned(right)], 0)
    return (times(left, packed) * W ** (-0.5)).astype(jnp.bfloat16)


def hop_of(mask):
    return mask >> 1 & 3


def swapped_slots(plan):
    return (hop_of(plan[0]) > hop_of(plan[1])).astype(jnp.int32)


def spectra_kernel(
    plan_ref, own_ref, got_ref, inside_ref, within_ref, round_ref, staged, within_sem, round_sem
):
    freqs = own_ref.shape[0]
    me = lax.axis_index("grp")
    swapped = swapped_slots(plan_ref)
    within_copy = pltpu.make_async_copy(inside_ref, within_ref.at[0], within_sem)
    within_copy.start()

    def round_copy(f, r):
        return pltpu.make_async_copy(staged.at[r, f], round_ref.at[0, r, f], round_sem.at[r, f])

    def make(f, carry):
        own = own_ref.at[f]
        for r in range(ROUNDS):
            partner = got_ref.at[swapped if r == 0 else 1 - swapped, f]
            lower = me < jnp.bitwise_xor(me, plan_ref[r])

            side = pl.multiple_of(jnp.where(lower, 0, 2 * GSTA), 2 * GSTA)
            for left, right, below, above in ((0, 2 * GSTA, 2, 0), (side, side, 0, 4)):
                rows = own[pl.ds(left, 2 * GSTA), :]
                for j in range(2):
                    product = cross(rows, partner[pl.ds(right + j * GSTA, GSTA), :])
                    for i in range(2):
                        k = jnp.where(lower, below + i * GPD + j, above + i * 2 + j)
                        staged[r, f, k] = product[i * GSTA : (i + 1) * GSTA]

            round_copy(f, r).start()
        return carry

    def finish(f, carry):
        for r in range(ROUNDS):
            round_copy(f, r).wait()
        return carry

    lax.fori_loop(0, freqs, make, 0)
    lax.fori_loop(0, freqs, finish, 0)
    within_copy.wait()


def spectra(plan, own, got, inside):
    freqs = own.shape[0]
    rounds = (ROUNDS, freqs, 8, GSTA, 2 * GSTA)
    dma = pltpu.SemaphoreType.DMA
    return pl.pallas_call(
        spectra_kernel,
        in_specs=[pl.BlockSpec(memory_space=pltpu.SMEM)] + [pl.BlockSpec(memory_space=pltpu.VMEM)] * 3,
        out_specs=[pl.BlockSpec(memory_space=pl.ANY)] * 2,
        out_shape=[
            jax.ShapeDtypeStruct((1,) + inside.shape, jnp.bfloat16),
            jax.ShapeDtypeStruct((1,) + rounds, jnp.bfloat16),
        ],
        scratch_shapes=[pltpu.VMEM(rounds, jnp.bfloat16), dma, dma((ROUNDS, freqs))],
        compiler_params=pltpu.CompilerParams(vmem_limit_bytes=36 * 1024 * 1024),
        cost_estimate=pl.CostEstimate(flops=5 * 10**9, bytes_accessed=14 * 10**6, transcendentals=0),
        name="spectra",
    )(plan, own, got, inside)


X_LO = 8
X_HI = 4
BANDS = 8
SLICES = 2


def flip(index, size):
    return index + size - 2 * size * (index // size % 2)


def meet(index, bits, size):
    for bit in (1, 2):
        if bits & bit:
            index = flip(index, size * bit)
    return index


def exchange_kernel(
    hops, pass_on, plan_ref, rec_ref, own_ref, got_ref, inside_ref,
    raw, ready, across, blocks, picked, mine, inside,
    raw_sem, z_out, z_in, x_out, x_in, core_out, core_in, y_out, y_in, own_sem, inside_sem,
):
    chunks = blocks.shape[0]
    swapped = swapped_slots(plan_ref)
    masks = [plan_ref[swapped], plan_ref[1 - swapped]]
    half = BANDS // 2
    g = lax.axis_index("grp")
    q = lax.axis_index("freq")
    z = q % 4
    hi = q // X_HI
    inner = (flip(g, X_LO), q)
    outer = (flip(g, X_LO), flip(q, X_HI))
    mate = (flip(g, 1), q)
    aside = [(g, meet(q, j, 1)) for j in range(1, 4)]
    along = [(meet(g, hop, 2), q) for hop in hops]
    sends = [r for r in range(ROUNDS) if not (pass_on and pass_on[1] == r)]
    friends = [inner, outer, mate] + aside + [along[r] for r in sends if hops[r]]
    if pass_on:
        first, second, turn, swap = pass_on
        onward = (meet(flip(g, 1) if swap else g, turn, 2), q)
        friends.append(onward)

    def raw_copy(c):
        return pltpu.make_async_copy(rec_ref.at[:, c], raw.at[c], raw_sem.at[c])

    def load(c, carry):
        raw_copy(c).start()
        return carry

    lax.fori_loop(0, chunks, load, 0)

    barrier = pltpu.get_barrier_semaphore()
    for friend in friends:
        pl.semaphore_signal(barrier, inc=1, device_id=friend, device_id_type=pl.DeviceIdType.MESH)
    pl.semaphore_wait(barrier, len(friends))

    near = pl.ds(hi * half, half)
    far = pl.ds((1 - hi) * half, half)

    def remote(source, target, sent, landed, device):
        return pltpu.make_async_remote_copy(
            src_ref=source, dst_ref=target, send_sem=sent, recv_sem=landed,
            device_id=device, device_id_type=pl.DeviceIdType.MESH,
        )

    def z_copies(c):
        copies = []
        for j in range(3):
            copies.append(remote(
                ready.at[c, j, 0], blocks.at[c, 0, 0, hi * half + z],
                z_out.at[c, j, 0], z_in.at[c, j, 0], aside[j],
            ))
            copies.append(remote(
                ready.at[c, j, 1], across.at[c, z],
                z_out.at[c, j, 1], z_in.at[c, j, 1], aside[j],
            ))
        return copies

    def x_inner(c):
        return remote(
            blocks.at[c, 0, 0, near], blocks.at[c, 0, 1, near], x_out.at[c, 0], x_in.at[c, 0], inner
        )

    def x_outer(c, rows):
        return remote(across.at[c], blocks.at[c, 0, 1, rows], x_out.at[c, 1], x_in.at[c, 1], outer)

    def x_relay(c):
        return remote(
            blocks.at[c, 0, 1, far], blocks.at[c, 0, 0, far], x_out.at[c, 2], x_in.at[c, 2], inner
        )

    def core_copy(c):
        return remote(blocks.at[c, 0], blocks.at[c, 1], core_out.at[c], core_in.at[c], mate)

    def own_copy(c):
        return pltpu.make_async_copy(
            blocks.at[c, 0, 0], own_ref.at[c // SLICES, :, c % SLICES], own_sem.at[c]
        )

    def landing(c, r):
        return got_ref.at[r, c // SLICES, :, c % SLICES]

    def y_copy(c, r):
        if hops[r]:
            return remote(
                picked.at[r, c], landing(c, r), y_out.at[r, c], y_in.at[r, c], along[r]
            )
        return pltpu.make_async_copy(picked.at[r, c], landing(c, r), y_out.at[r, c])

    def onward_copy(c):
        return remote(
            landing(c, first), landing(c, second), y_out.at[second, c], y_in.at[second, c], onward
        )

    def whiten(c):
        raw_copy(c).wait()
        for j in range(4):
            for k in range(2):
                band = (hi if k == 0 else 1 - hi) * half + meet(z, j, 1)
                values = raw[c, band].astype(jnp.float32)
                power = jnp.sum(values * values, -1, keepdims=True) / W
                white = (values * lax.rsqrt(power + EPS)).astype(jnp.bfloat16)
                if j:
                    ready[c, j - 1, k] = white
                elif k:
                    across[c, z] = white
                else:
                    blocks[c, 0, 0, hi * half + z] = white
        for copy in z_copies(c):
            copy.start()

    def spread(c):
        for copy in z_copies(c):
            copy.wait_recv()
        x_inner(c).start()
        x_outer(c, near).start()

    def relay(c):
        x_outer(c, far).wait_recv()
        x_relay(c).start()

    def share(c):
        x_inner(c).wait_recv()
        x_relay(c).wait_recv()
        core_copy(c).start()
        own_copy(c).start()

    def send(c):
        core_copy(c).wait_recv()
        for r in sends:
            other_lo = masks[r] >= X_LO
            other_core = masks[r] % 2 == 1
            here = jnp.where(other_lo, blocks[c, 0, 1], blocks[c, 0, 0])
            there = jnp.where(other_lo, blocks[c, 1, 1], blocks[c, 1, 0])
            picked[r, c] = jnp.where(other_core, there, here)
            y_copy(c, r).start()

    def hand_on(c):
        y_copy(c, first).wait_recv()
        onward_copy(c).start()

    def inside_copy(f):
        return pltpu.make_async_copy(inside.at[f], inside_ref.at[f], inside_sem.at[f])

    def pair_up(c):
        f = c // SLICES
        part = blocks.shape[-2]
        for p in range(BANDS):
            for piece in range(SLICES):
                start = (p * SLICES + piece) * part
                mine[start : start + part] = blocks[f * SLICES + piece, 0, 0, p]
        pairs = group_pairs()
        for j in range(GPD):
            product = cross(mine[: (j + 1) * GSTA], mine[j * GSTA : (j + 1) * GSTA])
            for i in range(j + 1):
                inside[f, pairs.index((i, j))] = product[i * GSTA : (i + 1) * GSTA]
        inside_copy(f).start()

    stages = [(whiten, 0), (spread, 1), (relay, 2), (share, 3), (send, 3)]
    if pass_on:
        stages.append((hand_on, 5))

    def step(t, carry):
        for stage, late in stages:
            pl.when((t >= late) & (t < chunks + late))(functools.partial(stage, t - late))
        done = t - 3
        pl.when((done >= 0) & (done < chunks) & (done % SLICES == SLICES - 1))(
            functools.partial(pair_up, done)
        )
        return carry

    lax.fori_loop(0, chunks + max(late for _, late in stages), step, 0)

    def finish(c, carry):
        for copy in z_copies(c) + [x_inner(c), x_outer(c, near), x_relay(c), core_copy(c)]:
            copy.wait_send()
        own_copy(c).wait()
        pl.when(c % SLICES == 0)(lambda: inside_copy(c // SLICES).wait())
        for r in sends:
            if pass_on and r == first:
                y_copy(c, r).wait_send()
            else:
                y_copy(c, r).wait()
        if pass_on:
            onward_copy(c).wait()
        return carry

    lax.fori_loop(0, chunks, finish, 0)


def exchange(records, plan, variant, number):
    freqs, stations, width = records.shape
    chunks = freqs // BANDS * SLICES
    part = (stations // SLICES, width)
    block = (BANDS,) + part
    dma = pltpu.SemaphoreType.DMA
    pairs = (len(group_pairs()), GSTA, 2 * GSTA)
    own, got, inside = pl.pallas_call(
        functools.partial(exchange_kernel, *variant),
        out_shape=[
            jax.ShapeDtypeStruct((freqs // BANDS, BANDS, SLICES) + part, jnp.bfloat16),
            jax.ShapeDtypeStruct((ROUNDS, freqs // BANDS, BANDS, SLICES) + part, jnp.bfloat16),
            jax.ShapeDtypeStruct((freqs // BANDS,) + pairs, jnp.bfloat16),
        ],
        in_specs=[pl.BlockSpec(memory_space=pltpu.SMEM), pl.BlockSpec(memory_space=pl.ANY)],
        out_specs=[pl.BlockSpec(memory_space=pl.ANY)] * 3,
        scratch_shapes=[
            pltpu.VMEM((chunks,) + block, jnp.bfloat16),
            pltpu.VMEM((chunks, 3, 2) + part, jnp.bfloat16),
            pltpu.VMEM((chunks, BANDS // 2) + part, jnp.bfloat16),
            pltpu.VMEM((chunks, 2, 2) + block, jnp.bfloat16),
            pltpu.VMEM((ROUNDS, chunks) + block, jnp.bfloat16),
            pltpu.VMEM((stations * BANDS, width), jnp.bfloat16),
            pltpu.VMEM((freqs // BANDS,) + pairs, jnp.bfloat16),
            dma((chunks,)),
            dma((chunks, 3, 2)), dma((chunks, 3, 2)), dma((chunks, 3)), dma((chunks, 3)),
            dma((chunks,)), dma((chunks,)), dma((ROUNDS, chunks)), dma((ROUNDS, chunks)),
            dma((chunks,)), dma((freqs // BANDS,)),
        ],
        compiler_params=pltpu.CompilerParams(
            collective_id=1 + number, has_side_effects=True, vmem_limit_bytes=46 * 1024 * 1024
        ),
        name="exchange_%d" % number,
    )(plan, records.reshape((BANDS, chunks) + part))
    shape = (freqs // BANDS, stations * BANDS, width)
    return own.reshape(shape), got.reshape((ROUNDS,) + shape), inside


def variants():
    found = [((low, high), None) for high in range(4) for low in range(high + 1)]
    found += [((hop, hop), (0, 1, 0, 1)) for hop in (1, 2, 3)]
    found += [((1, 2), (0, 1, 3, swap)) for swap in range(2)]
    found += [((2, 3), (1, 0, 1, swap)) for swap in range(2)]
    return found


def variant_number(plan):
    other = jnp.flip(plan)
    first, second = hop_of(plan), hop_of(other)
    low, high = jnp.minimum(first, second), jnp.maximum(first, second)
    change = plan ^ other
    direct = (high * (high + 1) >> 1) + low
    turned_off = 13 + ((high & 1) << 1) + (change & 1)
    relayed = jnp.where(low == high, 9 + high, turned_off)
    return jnp.where((change < X_LO) & (low != 0) & (low * high != 3), relayed, direct)[0]


def body(records, plan):
    branches = [
        functools.partial(exchange, variant=variant, number=number)
        for number, variant in enumerate(variants())
    ]
    return spectra(plan, *lax.switch(variant_number(plan), branches, records, plan))


def solution(mesh):
    placed = (P(None, ("grp", "freq"), None), P())
    return jax.shard_map(
        body,
        mesh=mesh,
        in_specs=placed,
        out_specs=(P("grp", "freq", None, None, None), P("grp", None, "freq", None, None, None)),
        check_vma=False,
    )
```
